32 devices in a mesh: seq: 8 (over z, x), tensor: 4 (over y, core).
Axes of the slice: x: 2, y: 2, z: 4, core: 2. Of those that a mesh axis runs over, the one named last changes fastest.
Arguments:
- features: bfloat16 [16, 7168], P(None, 'seq'), may hold values from -300 to 300
- input_norm_scale: float32 [7168], P('seq'), may hold values from 0.25 to 1.75
- query_key_value_weight: bfloat16 [7168, 3, 7168], P('seq', None, 'tensor'), may hold values from -0.0625 to 0.0625
- adapter_down_weight: bfloat16 [7168, 128], P('seq'), may hold values from -0.0625 to 0.0625
- adapter_up_weight: bfloat16 [128, 7168], P(None, 'tensor'), may hold values from -0.5 to 0.5
- output_weight: bfloat16 [7168, 3584], P('tensor', 'seq'), may hold values from -0.0625 to 0.0625
- cached_key_rows: bfloat16 [4, 4096, 7168], P(None, 'seq', 'tensor'), may hold values from -400 to 400
- cached_value_rows: bfloat16 [4, 4096, 7168], P(None, 'seq', 'tensor'), may hold values from -6 to 6
- lengths: int32 [4], replicated, may hold values from 16 to 4092, as said below
- sinks: int32 [4], replicated, may hold values from 1 to 4, as said below
- windows: int32 [4], replicated, may hold values from 512 to 1024, as said below
Outputs:
- mixed: float32 [16, 3584], P(None, 'seq')
- new_kv: float32 [2, 16, 7168], P(None, None, 'tensor')
The draws below stay inside these ranges and needn't reach their ends.
Inputs may be any that keep to these rules, and one draw needn't show every extreme that they name: `lengths`: heavy-tailed; at least one request has 4092. `sinks`: at least one request has 4. `windows`: at least one request has 1024.
All inputs are finite; a program needn't handle non-finite values.
Results may differ from the reference program's by a relative error of at most 0.022.
Values sent between devices are 32-bit elements; how exact they have to be, the bound alone decides.
A program may use at most 128 MiB of HBM per device.

```python
import math
import jax
import jax.numpy as jnp
from jax import lax

D = 3584
HEADS = 32
HD = 224
ADAPTER_RANK = 128
REQ = 4
NEW = 4
SINKS = 4
INPUT_WIDTH = 7168
ATTENTION_WIDTH = 7168
CTX = 4096
WINDOW = 1024
ROWS = 16


def lengths_common(key):
    sub = jax.random.fold_in(key, 11)
    first, second, third = jax.random.split(sub, 3)
    power = jax.random.randint(first, (REQ,), 4, int(math.log2(CTX)), dtype=jnp.int32)
    base = jnp.left_shift(jnp.ones((REQ,), jnp.int32), power)
    extra = jax.random.randint(second, (REQ,), 0, base, dtype=jnp.int32)
    longest = CTX - NEW
    length = jnp.minimum(base + extra, longest)
    forced = jax.random.randint(third, (), 0, REQ, dtype=jnp.int32)
    return jnp.where(jnp.arange(REQ, dtype=jnp.int32) == forced, longest, length).astype(jnp.int32)


def draw_lengths(key, part):
    return lengths_common(key)


def draw_sinks(key, part):
    first, second = jax.random.split(jax.random.fold_in(key, 12))
    count = jax.random.randint(first, (REQ,), 1, SINKS + 1, dtype=jnp.int32)
    forced = jax.random.randint(second, (), 0, REQ, dtype=jnp.int32)
    return jnp.where(jnp.arange(REQ, dtype=jnp.int32) == forced, SINKS, count).astype(jnp.int32)


def draw_windows(key, part):
    first, second = jax.random.split(jax.random.fold_in(key, 13))
    lowest = max(NEW + 2, WINDOW // 2)
    width = jax.random.randint(first, (REQ,), lowest, WINDOW + 1, dtype=jnp.int32)
    forced = jax.random.randint(second, (), 0, REQ, dtype=jnp.int32)
    return jnp.where(jnp.arange(REQ, dtype=jnp.int32) == forced, WINDOW, width).astype(jnp.int32)


def draw_cached_key_rows(key, part):
    sub = jax.random.fold_in(key, 21)
    position = jnp.arange(CTX, dtype=jnp.int32)
    lift = jnp.where(position < SINKS, 1.6, 1.0)[:, None]

    def one(index):
        inner = jax.random.fold_in(sub, index)
        base = jnp.clip(jax.random.normal(inner, (CTX, ATTENTION_WIDTH)), -6.0, 6.0) * 1.8 * lift
        return base.astype(jnp.bfloat16)
    return lax.map(one, jnp.arange(REQ, dtype=jnp.int32))


def draw_features(key, part):
    first, second, third = jax.random.split(jax.random.fold_in(key, 31), 3)
    column = jnp.arange(INPUT_WIDTH, dtype=jnp.float32)
    rising = jnp.exp(0.5 * math.log(3.0) * column / INPUT_WIDTH)
    col_scale = rising * jnp.exp(jax.random.uniform(first, (INPUT_WIDTH,), minval=0.0, maxval=math.log(10.0)))
    row_scale = jnp.exp(jax.random.uniform(second, (ROWS,), minval=math.log(0.3), maxval=math.log(3.0)))
    base = jnp.clip(jax.random.normal(third, (ROWS, INPUT_WIDTH)), -4.0, 4.0)
    return (base * row_scale[:, None] * col_scale[None, :]).astype(jnp.bfloat16)


def level_of(stream_key, dims, cuts, low, high):
    gain = 1.0
    for dim, shards_of in cuts:
        draws = jax.random.uniform(jax.random.fold_in(jax.random.fold_in(stream_key, 6), dim), (shards_of,), jnp.float32, low / len(cuts), high / len(cuts))
        gain = gain * jnp.repeat(jnp.exp(draws), dims[dim] // shards_of).reshape((-1,) + (1,) * (len(dims) - 1 - dim))
    return gain


def gaussian(rng, shape, spread, bound, pieces=(), held_as=jnp.bfloat16):
    gain = level_of(rng, shape, pieces, -0.22, 0.18) if pieces else 1.0
    values = jax.random.normal(rng, shape, jnp.float32) * spread * gain
    return jnp.minimum(jnp.maximum(values, -bound), bound).astype(held_as)


def setup_inputs(seed: int = 0) -> dict:
    key_of = jax.random.split(jax.random.key(seed), 12)
    features = draw_features(jax.random.fold_in(key_of[11], 71), 0)
    input_norm_scale = jnp.clip(1.0 + 0.15 * jax.random.normal(key_of[1], (INPUT_WIDTH,), jnp.float32), 0.25, 1.75)
    query_key_value_weight = gaussian(key_of[2], (INPUT_WIDTH, 3, ATTENTION_WIDTH), INPUT_WIDTH ** -0.5, 0.0625, ((0, 8), (2, 4)))
    adapter_down_weight = gaussian(key_of[3], (INPUT_WIDTH, ADAPTER_RANK), INPUT_WIDTH ** -0.5, 0.0625, ((0, 8),))
    adapter_up_weight = gaussian(key_of[4], (ADAPTER_RANK, ATTENTION_WIDTH), ADAPTER_RANK ** -0.5, 0.5, ((1, 4),))
    output_weight = gaussian(key_of[5], (ATTENTION_WIDTH, D), ATTENTION_WIDTH ** -0.5, 0.0625, ((0, 4), (1, 8)))
    cached_key_rows = draw_cached_key_rows(jax.random.fold_in(key_of[11], 71), 0)
    cached_value_rows = gaussian(key_of[7], (REQ, CTX, ATTENTION_WIDTH), 1.0, 6.0, ((1, 8), (2, 4)))
    lengths = draw_lengths(jax.random.fold_in(key_of[11], 71), 0)
    sinks = draw_sinks(jax.random.fold_in(key_of[11], 71), 0)
    windows = draw_windows(jax.random.fold_in(key_of[11], 71), 0)
    return dict(features=features, input_norm_scale=input_norm_scale, query_key_value_weight=query_key_value_weight, adapter_down_weight=adapter_down_weight, adapter_up_weight=adapter_up_weight, output_weight=output_weight, cached_key_rows=cached_key_rows, cached_value_rows=cached_value_rows, lengths=lengths, sinks=sinks, windows=windows)


NEG = -1e+30
CUT = -1e+29

def reference(features, input_norm_scale, query_key_value_weight, adapter_down_weight, adapter_up_weight, output_weight, cached_key_rows, cached_value_rows, lengths, sinks, windows):
    feat = features.astype(jnp.float32)
    mean_sq = lax.optimization_barrier(jnp.sum(feat * feat, axis=1)) / INPUT_WIDTH
    scale_rows = lax.rsqrt(mean_sq + 1e-05)[:, None]
    scaled_scores = (feat * input_norm_scale).astype(jnp.bfloat16)
    projected = jnp.dot(scaled_scores, query_key_value_weight.reshape(INPUT_WIDTH, 3 * ATTENTION_WIDTH), preferred_element_type=jnp.float32)
    low_rank_query = (jnp.dot(scaled_scores, adapter_down_weight, preferred_element_type=jnp.float32) * scale_rows).astype(jnp.bfloat16)
    query_adapter = jnp.dot(low_rank_query, adapter_up_weight, preferred_element_type=jnp.float32)
    queries = (projected[:, :ATTENTION_WIDTH] * scale_rows + query_adapter).astype(jnp.bfloat16)
    keys_full = projected[:, ATTENTION_WIDTH:2 * ATTENTION_WIDTH] * scale_rows
    values_full = projected[:, 2 * ATTENTION_WIDTH:] * scale_rows
    new_keys = keys_full.astype(jnp.bfloat16)
    new_values = values_full.astype(jnp.bfloat16)
    query_all = queries.astype(jnp.float32).reshape(REQ, NEW, HEADS, HD)
    key_all = new_keys.astype(jnp.float32).reshape(REQ, NEW, HEADS, HD)
    value_all = new_values.astype(jnp.float32).reshape(REQ, NEW, HEADS, HD)
    position = jnp.arange(CTX, dtype=jnp.int32)
    order = jnp.arange(NEW, dtype=jnp.int32)
    causal = order[:, None] >= order[None, :]

    def one_request(index):
        length = lengths[index]
        sink = sinks[index]
        window = windows[index]
        keys = lax.dynamic_index_in_dim(cached_key_rows, index, 0, False).astype(jnp.float32).reshape(CTX, HEADS, HD)
        values = lax.dynamic_index_in_dim(cached_value_rows, index, 0, False).astype(jnp.float32).reshape(CTX, HEADS, HD)
        query = lax.dynamic_index_in_dim(query_all, index, 0, False)
        own_key = lax.dynamic_index_in_dim(key_all, index, 0, False)
        own_value = lax.dynamic_index_in_dim(value_all, index, 0, False)
        seen = (position[None, :] < length) & ((position[None, :] < sink) | (length + order[:, None] - position[None, :] < window))
        cache_s = jnp.where(seen[None], jnp.einsum('thd,phd->htp', query, keys) * HD ** (-0.5), NEG)
        own_s = jnp.where(causal[None], jnp.einsum('thd,uhd->htu', query, own_key) * HD ** (-0.5), NEG)
        top = jnp.maximum(lax.optimization_barrier(jnp.max(cache_s, axis=-1)), lax.optimization_barrier(jnp.max(own_s, axis=-1)))
        cache_e = jnp.where(cache_s > CUT, jnp.exp(cache_s - top[..., None]), 0.0)
        own_e = jnp.where(own_s > CUT, jnp.exp(own_s - top[..., None]), 0.0)
        total = lax.optimization_barrier(jnp.sum(cache_e, axis=-1)) + lax.optimization_barrier(jnp.sum(own_e, axis=-1))
        combined = jnp.einsum('htp,phd->htd', cache_e.astype(jnp.bfloat16).astype(jnp.float32), values)
        combined = combined + jnp.einsum('htu,uhd->htd', own_e.astype(jnp.bfloat16).astype(jnp.float32), own_value)
        return (combined / total[..., None]).transpose(1, 0, 2).reshape(NEW, ATTENTION_WIDTH)
    attn = lax.map(one_request, jnp.arange(REQ, dtype=jnp.int32)).reshape(ROWS, ATTENTION_WIDTH).astype(jnp.bfloat16)
    mixed = jnp.dot(attn, output_weight, preferred_element_type=jnp.float32)
    return (mixed, jnp.stack([keys_full, values_full]))
```

```python
import functools

import jax
import jax.numpy as jnp
from jax import lax
from jax.experimental import pallas as pl
from jax.experimental.pallas import tpu as pltpu
from jax.sharding import PartitionSpec as P

HD = 224
NEW = 4
INPUT_WIDTH = 7168
PAD = 256
SIDE = 16

NEG = -1e30
CUT = -1e29
MESH = pl.DeviceIdType.MESH
F32 = jnp.float32
BF16 = jnp.bfloat16


def dot_t(a, b):
    return lax.dot_general(a, b, (((1,), (1,)), ((), ())), preferred_element_type=F32)


def block_kernel(
    seq, tensor, heads, count,
    x_hbm, g_hbm, w_hbm, down_hbm, up_hbm, wo_hbm, k_hbm, v_hbm, len_ref, sink_ref, win_ref,
    mixed_ref, kv_ref,
    x_v, g_v, w_v, down_v, up_v, wo_v, k_v, v_v,
    q_send, q_part, q_all, q_full, qblk,
    kv_send, kv_part, kv_all,
    o_full, m_full, l_full, o_send, o_part, a_all, a_full, t_part, prob, load_sem,
    q_ss, q_rs, qa_ss, qa_rs, kv_ss, kv_rs, kva_ss, kva_rs, o_ss, o_rs, a_ss, a_rs, t_ss, t_rs,
):
    me = lax.axis_index("seq")
    mine_t = lax.axis_index("tensor")
    per = seq // heads
    my_h = lax.div(me, jnp.int32(per))
    owner = lax.rem(me, jnp.int32(per)) == 0
    span = k_v.shape[1]
    rows = x_v.shape[0]
    group = NEW * heads

    def load(src, dst, index):
        return pltpu.make_async_copy(src, dst, load_sem.at[index])

    first = [load(x_hbm, x_v, 0), load(g_hbm, g_v, 1), load(w_hbm.at[0], w_v.at[0], 2),
             load(down_hbm, down_v, 3), load(up_hbm, up_v, 4)]
    rest = [load(w_hbm.at[1], w_v.at[1], 5), load(w_hbm.at[2], w_v.at[2], 6)]
    keys = [load(k_hbm.at[r], k_v.at[r], 8 + r) for r in range(count)]
    values = [load(v_hbm.at[r], v_v.at[r], 8 + count + r) for r in range(count)]
    wo_load = load(wo_hbm, wo_v, 7)
    for c in first:
        c.start()

    barrier = pltpu.get_barrier_semaphore()
    for d in range(1, seq):
        pl.semaphore_signal(barrier, inc=1, device_id={"seq": lax.rem(me + d, seq)}, device_id_type=MESH)
    for d in range(1, tensor):
        pl.semaphore_signal(barrier, inc=1, device_id={"tensor": lax.rem(mine_t + d, tensor)}, device_id_type=MESH)

    def on_owner(f):
        if per == 1:
            f()
        else:
            pl.when(owner)(f)

    def to_owners(src, dst, ss, rs, act):
        for d in range(1 if per == 1 else 0, heads):
            h = lax.rem(my_h + d, heads)

            def one(h=h, d=d):
                act(pltpu.make_async_remote_copy(
                    src_ref=src.at[h], dst_ref=dst.at[me], send_sem=ss.at[d], recv_sem=rs.at[me],
                    device_id={"seq": h * per}, device_id_type=MESH))

            if per == 1:
                one()
            else:
                pl.when(h * per != me)(one)

    def wait_parts(src, dst, rs, ss):
        for d in range(1, seq):
            s = lax.rem(me + d, seq)
            pltpu.make_async_remote_copy(
                src_ref=src.at[0], dst_ref=dst.at[s], send_sem=ss.at[0], recv_sem=rs.at[s],
                device_id={"seq": s}, device_id_type=MESH).wait_recv()

    def from_owner(buf, ss, rs, act):
        for d in range(1, seq):
            act(pltpu.make_async_remote_copy(
                src_ref=buf.at[my_h], dst_ref=buf.at[my_h], send_sem=ss.at[d], recv_sem=rs.at[my_h],
                device_id={"seq": lax.rem(me + d, seq)}, device_id_type=MESH))

    def wait_results(buf, ss, rs):
        for d in range(1 if per == 1 else 0, heads):
            h = lax.rem(my_h + d, heads)

            def one(h=h):
                pltpu.make_async_remote_copy(
                    src_ref=buf.at[h], dst_ref=buf.at[h], send_sem=ss.at[0], recv_sem=rs.at[h],
                    device_id={"seq": lax.rem(me + 1, seq)}, device_id_type=MESH).wait_recv()

            if per == 1:
                one()
            else:
                pl.when(h * per != me)(one)

    start = lambda c: c.start()
    wait_send = lambda c: c.wait_send()

    def head(h):
        return slice(h * HD, (h + 1) * HD)

    for c in first[:2]:
        c.wait()
    feat = x_v[...].astype(F32)
    scaled = (feat * g_v[...].reshape(1, feat.shape[1])).astype(BF16)
    sq = jnp.sum(feat * feat, axis=1, keepdims=True)
    first[2].wait()
    for c in rest:
        c.start()
    for c in keys:
        c.start()
    first[3].wait()
    first[4].wait()
    low = jnp.dot(scaled, down_v[...], preferred_element_type=F32)
    low_hi = low.astype(BF16)
    low_lo = (low - low_hi.astype(F32)).astype(BF16)
    q_partial = jnp.dot(scaled, w_v[0], preferred_element_type=F32)
    q_partial += jnp.dot(low_hi, up_v[...], preferred_element_type=F32)
    q_partial += jnp.dot(low_lo, up_v[...], preferred_element_type=F32)
    for h in range(heads):
        q_send[h, :, 0:HD] = q_partial[:, head(h)]
        q_send[h, :, HD:PAD] = jnp.broadcast_to(sq, (rows, PAD - HD))
    pl.semaphore_wait(barrier, seq + tensor - 2)
    to_owners(q_send, q_part, q_ss, q_rs, start)

    for c in values:
        c.start()
    wo_load.start()
    for j in range(2):
        rest[j].wait()
        part = jnp.dot(scaled, w_v[1 + j], preferred_element_type=F32)
        for h in range(heads):
            kv_send[h, j, :, 0:HD] = part[:, head(h)]
            kv_send[h, j, :, HD:PAD] = jnp.zeros((rows, PAD - HD), F32)

    def scale_of(total):
        return lax.rsqrt(total[:, HD:HD + 1] / INPUT_WIDTH + 1e-05)

    def sum_queries():
        q_part[me] = q_send[my_h]
        wait_parts(q_send, q_part, q_rs, q_ss)
        total = q_part[0]
        for s in range(1, seq):
            total = total + q_part[s]
        scale = scale_of(total)
        lane = lax.broadcasted_iota(jnp.int32, (rows, PAD), 1)
        q_all[my_h] = jnp.where(lane < HD, total * scale, scale)
        from_owner(q_all, qa_ss, qa_rs, start)

    on_owner(sum_queries)
    to_owners(kv_send, kv_part, kv_ss, kv_rs, start)
    wait_results(q_all, qa_ss, qa_rs)
    for h in range(heads):
        q_full[:, head(h)] = q_all[h, :, 0:HD]

    row = lax.broadcasted_iota(jnp.int32, (group, heads * HD), 0)
    col = lax.broadcasted_iota(jnp.int32, (group, heads * HD), 1)
    low_col = lax.div(row, jnp.int32(NEW)) * HD
    own_head = (col >= low_col) & (col < low_col + HD)

    def fold(full):
        kept = jnp.where(own_head, full, 0.0)
        eight = kept[0:8]
        for i in range(1, group // 8):
            eight = eight + kept[8 * i:8 * i + 8]
        return eight[0:NEW] + eight[NEW:2 * NEW]

    s_row = lax.rem(lax.broadcasted_iota(jnp.int32, (group, span), 0), jnp.int32(NEW))
    position = me * span + lax.broadcasted_iota(jnp.int32, (group, span), 1)
    width = heads * HD
    for r in range(count):
        four = q_full[NEW * r:NEW * (r + 1), :]
        eight = jnp.concatenate([four, four], axis=0)
        tall = jnp.concatenate([eight] * (group // 8), axis=0)
        qblk[r] = jnp.where(own_head, tall, 0.0).astype(BF16)
        keys[r].wait()
        raw = dot_t(qblk[r], k_v[r]) * HD ** (-0.5)
        length = len_ref[r]
        seen = (position < length) & (
            (position < sink_ref[r]) | (length + s_row - position < win_ref[r]))
        scores = jnp.where(seen, raw, NEG)
        top = jnp.max(scores, axis=1, keepdims=True)
        expo = jnp.where(seen, jnp.exp(scores - top), 0.0)
        total = jnp.sum(expo, axis=1, keepdims=True)
        prob[r] = expo.astype(BF16)
        m_full[NEW * r:NEW * (r + 1), :] = fold(jnp.broadcast_to(top, (group, width)))
        l_full[NEW * r:NEW * (r + 1), :] = fold(jnp.broadcast_to(total, (group, width)))

    def sum_new():
        kv_part[me] = kv_send[my_h]
        wait_parts(kv_send, kv_part, kv_rs, kv_ss)
        scale = q_all[my_h][:, HD:HD + 1]
        for j in range(2):
            total = kv_part[0, j]
            for s in range(1, seq):
                total = total + kv_part[s, j]
            kv_all[my_h, j] = total * scale
        from_owner(kv_all, kva_ss, kva_rs, start)

    on_owner(sum_new)

    for r in range(count):
        values[r].wait()
        out = jnp.dot(prob[r], v_v[r], preferred_element_type=F32)
        o_full[NEW * r:NEW * (r + 1), :] = fold(out)
    for h in range(heads):
        o_send[h, :, 0:HD] = o_full[:, head(h)]
        o_send[h, :, HD:HD + SIDE] = m_full[:, h * HD:h * HD + SIDE]
        o_send[h, :, HD + SIDE:PAD] = l_full[:, h * HD:h * HD + SIDE]
    to_owners(o_send, o_part, o_ss, o_rs, start)

    def merge():
        query = q_all[my_h][:, 0:HD].astype(BF16)
        key = kv_all[my_h, 0][:, 0:HD].astype(BF16)
        value = kv_all[my_h, 1][:, 0:HD].astype(BF16)
        token = lax.broadcasted_iota(jnp.int32, (rows, rows), 0)
        other = lax.broadcasted_iota(jnp.int32, (rows, rows), 1)
        seen = (lax.div(token, jnp.int32(NEW)) == lax.div(other, jnp.int32(NEW))) & (other <= token)
        fresh = jnp.where(seen, dot_t(query, key) * HD ** (-0.5), NEG)
        own_top = jnp.max(fresh, axis=1, keepdims=True)
        expo = jnp.where(seen, jnp.exp(fresh - own_top), 0.0)
        own_sum = jnp.sum(expo, axis=1, keepdims=True)
        own_out = jnp.dot(expo.astype(BF16), value, preferred_element_type=F32)
        o_part[me] = o_send[my_h]
        wait_parts(o_send, o_part, o_rs, o_ss)
        top = own_top
        for s in range(seq):
            top = jnp.maximum(top, o_part[s][:, HD:HD + 1])
        factor = jnp.exp(own_top - top)
        total = own_sum * factor
        out = own_out * factor
        for s in range(seq):
            piece = o_part[s]
            factor = jnp.exp(piece[:, HD:HD + 1] - top)
            out = out + piece[:, 0:HD] * factor
            total = total + piece[:, HD + SIDE:HD + SIDE + 1] * factor
        a_all[my_h, :, 0:HD] = out / total
        a_all[my_h, :, HD:PAD] = jnp.zeros((rows, PAD - HD), F32)
        from_owner(a_all, a_ss, a_rs, start)

    on_owner(merge)

    wait_results(kv_all, kva_ss, kva_rs)
    for h in range(heads):
        for j in range(2):
            kv_ref[j, :, head(h)] = kv_all[h, j, :, 0:HD]
    wo_load.wait()
    wait_results(a_all, a_ss, a_rs)
    for h in range(heads):
        a_full[:, head(h)] = a_all[h, :, 0:HD]
    t_part[mine_t] = dot_t(a_full[...].astype(BF16), wo_v[...])

    def to_tensor(d):
        return pltpu.make_async_remote_copy(
            src_ref=t_part.at[mine_t], dst_ref=t_part.at[mine_t], send_sem=t_ss.at[d],
            recv_sem=t_rs.at[mine_t], device_id={"tensor": lax.rem(mine_t + d, tensor)},
            device_id_type=MESH)

    for d in range(1, tensor):
        to_tensor(d).start()
    to_owners(q_send, q_part, q_ss, q_rs, wait_send)
    to_owners(kv_send, kv_part, kv_ss, kv_rs, wait_send)
    to_owners(o_send, o_part, o_ss, o_rs, wait_send)
    on_owner(lambda: from_owner(q_all, qa_ss, qa_rs, wait_send))
    on_owner(lambda: from_owner(kv_all, kva_ss, kva_rs, wait_send))
    on_owner(lambda: from_owner(a_all, a_ss, a_rs, wait_send))
    for d in range(1, tensor):
        s = lax.rem(mine_t + d, tensor)
        pltpu.make_async_remote_copy(
            src_ref=t_part.at[s], dst_ref=t_part.at[s], send_sem=t_ss.at[0], recv_sem=t_rs.at[s],
            device_id={"tensor": s}, device_id_type=MESH).wait_recv()
    mixed = t_part[0]
    for s in range(1, tensor):
        mixed = mixed + t_part[s]
    mixed_ref[...] = mixed
    for d in range(1, tensor):
        to_tensor(d).wait_send()


def shards(
    seq, tensor,
    features, input_norm_scale, query_key_value_weight, adapter_down_weight, adapter_up_weight,
    output_weight, cached_key_rows, cached_value_rows, lengths, sinks, windows,
):
    rows, depth = features.shape
    count, span, width = cached_key_rows.shape
    heads = width // HD
    out_width = output_weight.shape[1]
    group = NEW * heads
    weights = jnp.transpose(query_key_value_weight, (1, 0, 2))
    wo = jnp.transpose(output_weight)
    hbm = pl.BlockSpec(memory_space=pltpu.HBM)
    smem = pl.BlockSpec(memory_space=pltpu.SMEM)
    vmem = pl.BlockSpec(memory_space=pltpu.VMEM)

    def like(a):
        return pltpu.VMEM(a.shape, a.dtype)

    dma = lambda n: pltpu.SemaphoreType.DMA((n,))
    ring = max(seq, heads)
    return pl.pallas_call(
        functools.partial(block_kernel, seq, tensor, heads, count),
        out_shape=(
            jax.ShapeDtypeStruct((rows, out_width), F32),
            jax.ShapeDtypeStruct((2, rows, width), F32),
        ),
        in_specs=[hbm] * 8 + [smem] * 3,
        out_specs=(vmem, vmem),
        scratch_shapes=[
            like(features), like(input_norm_scale), like(weights), like(adapter_down_weight),
            like(adapter_up_weight), like(wo), like(cached_key_rows), like(cached_value_rows),
            pltpu.VMEM((heads, rows, PAD), F32),
            pltpu.VMEM((seq, rows, PAD), F32),
            pltpu.VMEM((heads, rows, PAD), F32),
            pltpu.VMEM((rows, width), F32),
            pltpu.VMEM((count, group, width), BF16),
            pltpu.VMEM((heads, 2, rows, PAD), F32),
            pltpu.VMEM((seq, 2, rows, PAD), F32),
            pltpu.VMEM((heads, 2, rows, PAD), F32),
            pltpu.VMEM((rows, width), F32),
            pltpu.VMEM((rows, width), F32),
            pltpu.VMEM((rows, width), F32),
            pltpu.VMEM((heads, rows, PAD), F32),
            pltpu.VMEM((seq, rows, PAD), F32),
            pltpu.VMEM((heads, rows, PAD), F32),
            pltpu.VMEM((rows, width), F32),
            pltpu.VMEM((tensor, rows, out_width), F32),
            pltpu.VMEM((count, group, span), BF16),
            dma(8 + 2 * count),
        ] + [dma(ring)] * 12 + [dma(tensor)] * 2,
        compiler_params=pltpu.CompilerParams(
            collective_id=0, has_side_effects=True, vmem_limit_bytes=60 * 1024 * 1024,
        ),
    )(
        features, input_norm_scale, weights, adapter_down_weight, adapter_up_weight, wo,
        cached_key_rows, cached_value_rows, lengths, sinks, windows,
    )


def solution(mesh):
    in_specs = (
        P(None, "seq"),
        P("seq"),
        P("seq", None, "tensor"),
        P("seq", None),
        P(None, "tensor"),
        P("tensor", "seq"),
        P(None, "seq", "tensor"),
        P(None, "seq", "tensor"),
        P(),
        P(),
        P(),
    )
    out_specs = (P(None, "seq"), P(None, None, "tensor"))
    body = functools.partial(shards, mesh.shape["seq"], mesh.shape["tensor"])
    return jax.shard_map(body, mesh=mesh, in_specs=in_specs, out_specs=out_specs, check_vma=False)
```

```python
import functools

import jax
import jax.numpy as jnp
from jax import lax
from jax.experimental import pallas as pl
from jax.experimental.pallas import tpu as pltpu
from jax.sharding import PartitionSpec as P

HD = 224
NEW = 4
INPUT_WIDTH = 7168
PAD = 256
SIDE = 16

NEG = -1e30
CUT = -1e29
MESH = pl.DeviceIdType.MESH
F32 = jnp.float32
BF16 = jnp.bfloat16


def dot_t(a, b):
    return lax.dot_general(a, b, (((1,), (1,)), ((), ())), preferred_element_type=F32)


def block_kernel(
    seq, tensor, heads, count,
    x_hbm, g_hbm, w_hbm, down_hbm, up_hbm, wo_hbm, k_hbm, v_hbm, len_hbm, sink_hbm, win_hbm,
    mixed_ref, kv_ref,
    len_ref, sink_ref, win_ref,
    x_v, g_v, w_v, down_v, up_v, wo_v, k_v, v_v,
    q_send, q_part, q_all, q_full, qblk,
    kv_send, kv_mid, kv_sum, kv_part, kv_all,
    o_full, m_full, l_full, o_send, o_part, a_all, a_full, t_part, prob, load_sem,
    q_ss, q_rs, qa_ss, qa_rs, kvm_ss, kvm_rs, kv_ss, kv_rs, kva_ss, kva_rs, o_ss, o_rs, a_ss, a_rs, t_ss, t_rs,
):
    me = lax.axis_index("seq")
    mine_t = lax.axis_index("tensor")
    per = seq // heads
    my_h = lax.div(me, jnp.int32(per))
    owner = lax.rem(me, jnp.int32(per)) == 0
    span = k_v.shape[1]
    rows = x_v.shape[0]
    group = NEW * heads

    def load(src, dst, index):
        return pltpu.make_async_copy(src, dst, load_sem.at[index])

    first = [load(x_hbm, x_v, 0), load(g_hbm, g_v, 1), load(w_hbm.at[0], w_v.at[0], 2),
             load(down_hbm, down_v, 3), load(up_hbm, up_v, 4)]
    rest = [load(w_hbm.at[1], w_v.at[1], 5), load(w_hbm.at[2], w_v.at[2], 6)]
    keys = [load(k_hbm.at[r], k_v.at[r], 8 + r) for r in range(count)]
    values = [load(v_hbm.at[r], v_v.at[r], 8 + count + r) for r in range(count)]
    wo_load = load(wo_hbm, wo_v, 7)
    places = [load(a, b, 8 + 2 * count + i) for i, (a, b) in enumerate(
        ((len_hbm, len_ref), (sink_hbm, sink_ref), (win_hbm, win_ref)))]
    for c in first + places:
        c.start()

    barrier = pltpu.get_barrier_semaphore()
    for d in range(1, seq):
        pl.semaphore_signal(barrier, inc=1, device_id={"seq": lax.rem(me + d, seq)}, device_id_type=MESH)
    for d in range(1, tensor):
        pl.semaphore_signal(barrier, inc=1, device_id={"tensor": lax.rem(mine_t + d, tensor)}, device_id_type=MESH)

    def on_owner(f):
        if per == 1:
            f()
        else:
            pl.when(owner)(f)

    def to_owners(src, dst, ss, rs, act):
        for d in range(1 if per == 1 else 0, heads):
            h = lax.rem(my_h + d, heads)

            def one(h=h, d=d):
                act(pltpu.make_async_remote_copy(
                    src_ref=src.at[h], dst_ref=dst.at[me], send_sem=ss.at[d], recv_sem=rs.at[me],
                    device_id={"seq": h * per}, device_id_type=MESH))

            if per == 1:
                one()
            else:
                pl.when(h * per != me)(one)

    def wait_parts(src, dst, rs, ss):
        for d in range(1, seq):
            s = lax.rem(me + d, seq)
            pltpu.make_async_remote_copy(
                src_ref=src.at[0], dst_ref=dst.at[s], send_sem=ss.at[0], recv_sem=rs.at[s],
                device_id={"seq": s}, device_id_type=MESH).wait_recv()

    def from_owner(buf, ss, rs, act):
        for d in range(1, seq):
            act(pltpu.make_async_remote_copy(
                src_ref=buf.at[my_h], dst_ref=buf.at[my_h], send_sem=ss.at[d], recv_sem=rs.at[my_h],
                device_id={"seq": lax.rem(me + d, seq)}, device_id_type=MESH))

    def wait_results(buf, ss, rs):
        for d in range(1 if per == 1 else 0, heads):
            h = lax.rem(my_h + d, heads)

            def one(h=h):
                pltpu.make_async_remote_copy(
                    src_ref=buf.at[h], dst_ref=buf.at[h], send_sem=ss.at[0], recv_sem=rs.at[h],
                    device_id={"seq": lax.rem(me + 1, seq)}, device_id_type=MESH).wait_recv()

            if per == 1:
                one()
            else:
                pl.when(h * per != me)(one)

    start = lambda c: c.start()
    wait_send = lambda c: c.wait_send()

    def head(h):
        return slice(h * HD, (h + 1) * HD)

    for c in first[:2]:
        c.wait()
    feat = x_v[...].astype(F32)
    scaled = (feat * g_v[...].reshape(1, feat.shape[1])).astype(BF16)
    sq = jnp.sum(feat * feat, axis=1, keepdims=True)
    first[2].wait()
    for c in rest:
        c.start()
    for c in keys:
        c.start()
    first[3].wait()
    first[4].wait()
    low = jnp.dot(scaled, down_v[...], preferred_element_type=F32)
    low_hi = low.astype(BF16)
    low_lo = (low - low_hi.astype(F32)).astype(BF16)
    q_partial = jnp.dot(scaled, w_v[0], preferred_element_type=F32)
    q_partial += jnp.dot(low_hi, up_v[...], preferred_element_type=F32)
    q_partial += jnp.dot(low_lo, up_v[...], preferred_element_type=F32)
    for h in range(heads):
        q_send[h, :, 0:HD] = q_partial[:, head(h)]
        q_send[h, :, HD:PAD] = jnp.broadcast_to(sq, (rows, PAD - HD))
    pl.semaphore_wait(barrier, seq + tensor - 2)
    to_owners(q_send, q_part, q_ss, q_rs, start)

    for c in values:
        c.start()
    wo_load.start()
    paired = per == 1 and seq % 2 == 0
    half = heads // 2
    side = lax.rem(me, jnp.int32(2))
    partner = me + 1 - 2 * side

    def place(h):
        return h % 2 * half + h // 2 if paired else h

    for j in range(2):
        rest[j].wait()
        part = jnp.dot(scaled, w_v[1 + j], preferred_element_type=F32)
        for h in range(heads):
            kv_send[place(h), j, :, 0:HD] = part[:, head(h)]
            kv_send[place(h), j, :, HD:PAD] = jnp.zeros((rows, PAD - HD), F32)

    def scale_of(total):
        return lax.rsqrt(total[:, HD:HD + 1] / INPUT_WIDTH + 1e-05)

    def sum_queries():
        q_part[me] = q_send[my_h]
        wait_parts(q_send, q_part, q_rs, q_ss)
        total = q_part[0]
        for s in range(1, seq):
            total = total + q_part[s]
        scale = scale_of(total)
        lane = lax.broadcasted_iota(jnp.int32, (rows, PAD), 1)
        q_all[my_h] = jnp.where(lane < HD, total * scale, scale)
        from_owner(q_all, qa_ss, qa_rs, start)

    on_owner(sum_queries)

    def pair_parts():
        return pltpu.make_async_remote_copy(
            src_ref=kv_send.at[pl.ds((1 - side) * half, half)], dst_ref=kv_mid,
            send_sem=kvm_ss.at[0], recv_sem=kvm_rs.at[0],
            device_id={"seq": partner}, device_id_type=MESH)

    def pair_sums(d):
        owner_at = lax.rem(me + 2 * d, seq)
        return pltpu.make_async_remote_copy(
            src_ref=kv_sum.at[lax.div(owner_at, jnp.int32(2))],
            dst_ref=kv_part.at[lax.div(me, jnp.int32(2))],
            send_sem=kv_ss.at[d], recv_sem=kv_rs.at[lax.div(me, jnp.int32(2))],
            device_id={"seq": owner_at}, device_id_type=MESH)

    def spread(d):
        to = partner if d == 0 else lax.rem(me + 2 * d, seq)
        return pltpu.make_async_remote_copy(
            src_ref=kv_all.at[me], dst_ref=kv_all.at[me], send_sem=kva_ss.at[d],
            recv_sem=kva_rs.at[me], device_id={"seq": to}, device_id_type=MESH)

    def forward(d):
        h = lax.rem(me + 2 * d, seq)
        return pltpu.make_async_remote_copy(
            src_ref=kv_all.at[h], dst_ref=kv_all.at[h], send_sem=kva_ss.at[half + d - 1],
            recv_sem=kva_rs.at[h], device_id={"seq": partner}, device_id_type=MESH)

    def arrived(h):
        pltpu.make_async_remote_copy(
            src_ref=kv_all.at[h], dst_ref=kv_all.at[h], send_sem=kva_ss.at[0],
            recv_sem=kva_rs.at[h], device_id={"seq": partner}, device_id_type=MESH).wait_recv()

    if paired:
        pair_parts().start()
    else:
        to_owners(kv_send, kv_part, kv_ss, kv_rs, start)
    wait_results(q_all, qa_ss, qa_rs)
    for h in range(heads):
        q_full[:, head(h)] = q_all[h, :, 0:HD]

    row = lax.broadcasted_iota(jnp.int32, (group, heads * HD), 0)
    col = lax.broadcasted_iota(jnp.int32, (group, heads * HD), 1)
    low_col = lax.div(row, jnp.int32(NEW)) * HD
    own_head = (col >= low_col) & (col < low_col + HD)

    def fold(full):
        kept = jnp.where(own_head, full, 0.0)
        eight = kept[0:8]
        for i in range(1, group // 8):
            eight = eight + kept[8 * i:8 * i + 8]
        return eight[0:NEW] + eight[NEW:2 * NEW]

    s_row = lax.rem(lax.broadcasted_iota(jnp.int32, (group, span), 0), jnp.int32(NEW))
    position = me * span + lax.broadcasted_iota(jnp.int32, (group, span), 1)
    width = heads * HD
    for r in range(count):
        four = q_full[NEW * r:NEW * (r + 1), :]
        eight = jnp.concatenate([four, four], axis=0)
        tall = jnp.concatenate([eight] * (group // 8), axis=0)
        qblk[r] = jnp.where(own_head, tall, 0.0).astype(BF16)
        if r == 0:
            for c in places:
                c.wait()
        keys[r].wait()
        raw = dot_t(qblk[r], k_v[r]) * HD ** (-0.5)
        length = len_ref[r]
        seen = (position < length) & (
            (position < sink_ref[r]) | (length + s_row - position < win_ref[r]))
        scores = jnp.where(seen, raw, NEG)
        top = jnp.max(scores, axis=1, keepdims=True)
        expo = jnp.where(seen, jnp.exp(scores - top), 0.0)
        total = jnp.sum(expo, axis=1, keepdims=True)
        prob[r] = expo.astype(BF16)
        m_full[NEW * r:NEW * (r + 1), :] = fold(jnp.broadcast_to(top, (group, width)))
        l_full[NEW * r:NEW * (r + 1), :] = fold(jnp.broadcast_to(total, (group, width)))
        if paired and r == 0:
            pair_parts().wait_recv()
            for i in range(half):
                kv_sum[i] = kv_mid[i] + kv_send[side * half + i]
            for d in range(1, half):
                pair_sums(d).start()

    def sum_new():
        if paired:
            kv_part[lax.div(me, jnp.int32(2))] = kv_sum[lax.div(me, jnp.int32(2))]
            for d in range(1, half):
                s = lax.div(lax.rem(me + 2 * d, seq), jnp.int32(2))
                pltpu.make_async_remote_copy(
                    src_ref=kv_sum.at[0], dst_ref=kv_part.at[s], send_sem=kv_ss.at[0],
                    recv_sem=kv_rs.at[s], device_id={"seq": partner},
                    device_id_type=MESH).wait_recv()
        else:
            kv_part[me] = kv_send[my_h]
            wait_parts(kv_send, kv_part, kv_rs, kv_ss)
        scale = q_all[my_h][:, HD:HD + 1]
        for j in range(2):
            total = kv_part[0, j]
            for s in range(1, half if paired else seq):
                total = total + kv_part[s, j]
            kv_all[my_h, j] = total * scale
        if paired:
            for d in range(half):
                spread(d).start()
        else:
            from_owner(kv_all, kva_ss, kva_rs, start)

    on_owner(sum_new)

    for r in range(count):
        values[r].wait()
        out = jnp.dot(prob[r], v_v[r], preferred_element_type=F32)
        o_full[NEW * r:NEW * (r + 1), :] = fold(out)
    for h in range(heads):
        o_send[h, :, 0:HD] = o_full[:, head(h)]
        o_send[h, :, HD:HD + SIDE] = m_full[:, h * HD:h * HD + SIDE]
        o_send[h, :, HD + SIDE:PAD] = l_full[:, h * HD:h * HD + SIDE]
    to_owners(o_send, o_part, o_ss, o_rs, start)
    if paired:
        for d in range(1, half):
            arrived(lax.rem(me + 2 * d, seq))
            forward(d).start()

    def merge():
        query = q_all[my_h][:, 0:HD].astype(BF16)
        key = kv_all[my_h, 0][:, 0:HD].astype(BF16)
        value = kv_all[my_h, 1][:, 0:HD].astype(BF16)
        token = lax.broadcasted_iota(jnp.int32, (rows, rows), 0)
        other = lax.broadcasted_iota(jnp.int32, (rows, rows), 1)
        seen = (lax.div(token, jnp.int32(NEW)) == lax.div(other, jnp.int32(NEW))) & (other <= token)
        fresh = jnp.where(seen, dot_t(query, key) * HD ** (-0.5), NEG)
        own_top = jnp.max(fresh, axis=1, keepdims=True)
        expo = jnp.where(seen, jnp.exp(fresh - own_top), 0.0)
        own_sum = jnp.sum(expo, axis=1, keepdims=True)
        own_out = jnp.dot(expo.astype(BF16), value, preferred_element_type=F32)
        o_part[me] = o_send[my_h]
        wait_parts(o_send, o_part, o_rs, o_ss)
        top = own_top
        for s in range(seq):
            top = jnp.maximum(top, o_part[s][:, HD:HD + 1])
        factor = jnp.exp(own_top - top)
        total = own_sum * factor
        out = own_out * factor
        for s in range(seq):
            piece = o_part[s]
            factor = jnp.exp(piece[:, HD:HD + 1] - top)
            out = out + piece[:, 0:HD] * factor
            total = total + piece[:, HD + SIDE:HD + SIDE + 1] * factor
        a_all[my_h, :, 0:HD] = out / total
        a_all[my_h, :, HD:PAD] = jnp.zeros((rows, PAD - HD), F32)
        from_owner(a_all, a_ss, a_rs, start)

    on_owner(merge)

    if paired:
        for d in range(half):
            arrived(lax.rem(partner + 2 * d, seq))
    else:
        wait_results(kv_all, kva_ss, kva_rs)
    for h in range(heads):
        for j in range(2):
            kv_ref[j, :, head(h)] = kv_all[h, j, :, 0:HD]
    wo_load.wait()
    wait_results(a_all, a_ss, a_rs)
    for h in range(heads):
        a_full[:, head(h)] = a_all[h, :, 0:HD]
    t_part[mine_t] = dot_t(a_full[...].astype(BF16), wo_v[...])

    def to_tensor(d):
        return pltpu.make_async_remote_copy(
            src_ref=t_part.at[mine_t], dst_ref=t_part.at[mine_t], send_sem=t_ss.at[d],
            recv_sem=t_rs.at[mine_t], device_id={"tensor": lax.rem(mine_t + d, tensor)},
            device_id_type=MESH)

    for d in range(1, tensor):
        to_tensor(d).start()
    to_owners(q_send, q_part, q_ss, q_rs, wait_send)
    to_owners(o_send, o_part, o_ss, o_rs, wait_send)
    on_owner(lambda: from_owner(q_all, qa_ss, qa_rs, wait_send))
    if paired:
        pair_parts().wait_send()
        for d in range(1, half):
            pair_sums(d).wait_send()
            forward(d).wait_send()
        for d in range(half):
            spread(d).wait_send()
    else:
        to_owners(kv_send, kv_part, kv_ss, kv_rs, wait_send)
        on_owner(lambda: from_owner(kv_all, kva_ss, kva_rs, wait_send))
    on_owner(lambda: from_owner(a_all, a_ss, a_rs, wait_send))
    for d in range(1, tensor):
        s = lax.rem(mine_t + d, tensor)
        pltpu.make_async_remote_copy(
            src_ref=t_part.at[s], dst_ref=t_part.at[s], send_sem=t_ss.at[0], recv_sem=t_rs.at[s],
            device_id={"tensor": s}, device_id_type=MESH).wait_recv()
    mixed = t_part[0]
    for s in range(1, tensor):
        mixed = mixed + t_part[s]
    mixed_ref[...] = mixed
    for d in range(1, tensor):
        to_tensor(d).wait_send()


def shards(
    seq, tensor,
    features, input_norm_scale, query_key_value_weight, adapter_down_weight, adapter_up_weight,
    output_weight, cached_key_rows, cached_value_rows, lengths, sinks, windows,
):
    rows, depth = features.shape
    count, span, width = cached_key_rows.shape
    heads = width // HD
    out_width = output_weight.shape[1]
    group = NEW * heads
    weights = jnp.transpose(query_key_value_weight, (1, 0, 2))
    wo = jnp.transpose(output_weight)
    hbm = pl.BlockSpec(memory_space=pltpu.HBM)
    vmem = pl.BlockSpec(memory_space=pltpu.VMEM)

    def like(a):
        return pltpu.VMEM(a.shape, a.dtype)

    dma = lambda n: pltpu.SemaphoreType.DMA((n,))
    ring = max(seq, heads)
    return pl.pallas_call(
        functools.partial(block_kernel, seq, tensor, heads, count),
        out_shape=(
            jax.ShapeDtypeStruct((rows, out_width), F32),
            jax.ShapeDtypeStruct((2, rows, width), F32),
        ),
        in_specs=[hbm] * 11,
        out_specs=(vmem, vmem),
        scratch_shapes=[pltpu.SMEM((count,), jnp.int32)] * 3 + [
            like(features), like(input_norm_scale), like(weights), like(adapter_down_weight),
            like(adapter_up_weight), like(wo), like(cached_key_rows), like(cached_value_rows),
            pltpu.VMEM((heads, rows, PAD), F32),
            pltpu.VMEM((seq, rows, PAD), F32),
            pltpu.VMEM((heads, rows, PAD), F32),
            pltpu.VMEM((rows, width), F32),
            pltpu.VMEM((count, group, width), BF16),
            pltpu.VMEM((heads, 2, rows, PAD), F32),
            pltpu.VMEM((heads // 2, 2, rows, PAD), F32),
            pltpu.VMEM((heads // 2, 2, rows, PAD), F32),
            pltpu.VMEM((seq, 2, rows, PAD), F32),
            pltpu.VMEM((heads, 2, rows, PAD), F32),
            pltpu.VMEM((rows, width), F32),
            pltpu.VMEM((rows, width), F32),
            pltpu.VMEM((rows, width), F32),
            pltpu.VMEM((heads, rows, PAD), F32),
            pltpu.VMEM((seq, rows, PAD), F32),
            pltpu.VMEM((heads, rows, PAD), F32),
            pltpu.VMEM((rows, width), F32),
            pltpu.VMEM((tensor, rows, out_width), F32),
            pltpu.VMEM((count, group, span), BF16),
            dma(11 + 2 * count),
        ] + [dma(ring)] * 4 + [dma(1)] * 2 + [dma(ring)] * 8 + [dma(tensor)] * 2,
        compiler_params=pltpu.CompilerParams(
            collective_id=0, has_side_effects=True, vmem_limit_bytes=60 * 1024 * 1024,
        ),
    )(
        features, input_norm_scale, weights, adapter_down_weight, adapter_up_weight, wo,
        cached_key_rows, cached_value_rows, lengths, sinks, windows,
    )


def solution(mesh):
    in_specs = (
        P(None, "seq"),
        P("seq"),
        P("seq", None, "tensor"),
        P("seq", None),
        P(None, "tensor"),
        P("tensor", "seq"),
        P(None, "seq", "tensor"),
        P(None, "seq", "tensor"),
        P(),
        P(),
        P(),
    )
    out_specs = (P(None, "seq"), P(None, None, "tensor"))
    body = functools.partial(shards, mesh.shape["seq"], mesh.shape["tensor"])
    return jax.shard_map(body, mesh=mesh, in_specs=in_specs, out_specs=out_specs, check_vma=False)
```

```python
import functools

import jax
import jax.numpy as jnp
from jax import lax
from jax.experimental import pallas as pl
from jax.experimental.pallas import tpu as pltpu
from jax.sharding import PartitionSpec as P

HD = 224
NEW = 4
INPUT_WIDTH = 7168
PAD = 256
SIDE = 16

NEG = -1e30
CUT = -1e29
MESH = pl.DeviceIdType.MESH
F32 = jnp.float32
BF16 = jnp.bfloat16


def dot_t(a, b):
    return lax.dot_general(a, b, (((1,), (1,)), ((), ())), preferred_element_type=F32)


def block_kernel(
    seq, tensor, heads, count,
    x_hbm, g_hbm, w_hbm, down_hbm, up_hbm, wo_hbm, k_hbm, v_hbm, len_hbm, sink_hbm, win_hbm,
    mixed_ref, kv_ref,
    len_ref, sink_ref, win_ref,
    x_v, g_v, w_v, down_v, up_v, wo_v, k_v, v_v,
    q_send, q_part, q_all, q_full,
    kv_send, kv_mid, kv_sum, kv_part, kv_all,
    o_send, o_part, a_all, a_full, t_part, load_sem,
    q_ss, q_rs, qa_ss, qa_rs, kvm_ss, kvm_rs, kv_ss, kv_rs, kva_ss, kva_rs, o_ss, o_rs, a_ss, a_rs, t_ss, t_rs,
):
    me = lax.axis_index("seq")
    mine_t = lax.axis_index("tensor")
    per = seq // heads
    my_h = lax.div(me, jnp.int32(per))
    owner = lax.rem(me, jnp.int32(per)) == 0
    span = k_v.shape[1]
    rows = x_v.shape[0]
    group = NEW * heads
    halves = rows // 8
    each = count // halves

    def load(src, dst, index):
        return pltpu.make_async_copy(src, dst, load_sem.at[index])

    first = [load(x_hbm, x_v, 0), load(g_hbm, g_v, 1), load(w_hbm.at[0], w_v.at[0], 2),
             load(down_hbm, down_v, 3), load(up_hbm, up_v, 4)]
    rest = [load(w_hbm.at[1], w_v.at[1], 5), load(w_hbm.at[2], w_v.at[2], 6)]
    keys = [load(k_hbm.at[r], k_v.at[r], 8 + r) for r in range(count)]
    values = [load(v_hbm.at[r], v_v.at[r], 8 + count + r) for r in range(count)]
    wo_load = load(wo_hbm, wo_v, 7)
    places = [load(a, b, 8 + 2 * count + i) for i, (a, b) in enumerate(
        ((len_hbm, len_ref), (sink_hbm, sink_ref), (win_hbm, win_ref)))]
    for c in first + places:
        c.start()

    barrier = pltpu.get_barrier_semaphore()
    for d in range(1, seq):
        pl.semaphore_signal(barrier, inc=1, device_id={"seq": lax.rem(me + d, seq)}, device_id_type=MESH)
    for d in range(1, tensor):
        pl.semaphore_signal(barrier, inc=1, device_id={"tensor": lax.rem(mine_t + d, tensor)}, device_id_type=MESH)

    def on_owner(f):
        if per == 1:
            f()
        else:
            pl.when(owner)(f)

    ring = max(seq, heads)

    def view(ref, index, g):
        return ref.at[index] if g is None else ref.at[index, pl.ds(8 * g, 8)]

    def slot(index, g):
        return index if g is None else g * ring + index

    def to_owners(src, dst, ss, rs, act, g=None):
        for d in range(1 if per == 1 else 0, heads):
            h = lax.rem(my_h + d, heads)

            def one(h=h, d=d):
                act(pltpu.make_async_remote_copy(
                    src_ref=view(src, h, g), dst_ref=view(dst, me, g),
                    send_sem=ss.at[slot(d, g)], recv_sem=rs.at[slot(me, g)],
                    device_id={"seq": h * per}, device_id_type=MESH))

            if per == 1:
                one()
            else:
                pl.when(h * per != me)(one)

    def wait_parts(src, dst, rs, ss, g=None):
        for d in range(1, seq):
            s = lax.rem(me + d, seq)
            pltpu.make_async_remote_copy(
                src_ref=view(src, 0, g), dst_ref=view(dst, s, g),
                send_sem=ss.at[0], recv_sem=rs.at[slot(s, g)],
                device_id={"seq": s}, device_id_type=MESH).wait_recv()

    def from_owner(buf, ss, rs, act, g=None):
        for d in range(1, seq):
            act(pltpu.make_async_remote_copy(
                src_ref=view(buf, my_h, g), dst_ref=view(buf, my_h, g),
                send_sem=ss.at[slot(d, g)], recv_sem=rs.at[slot(my_h, g)],
                device_id={"seq": lax.rem(me + d, seq)}, device_id_type=MESH))

    def wait_results(buf, ss, rs, g=None):
        for d in range(1 if per == 1 else 0, heads):
            h = lax.rem(my_h + d, heads)

            def one(h=h):
                pltpu.make_async_remote_copy(
                    src_ref=view(buf, h, g), dst_ref=view(buf, h, g),
                    send_sem=ss.at[0], recv_sem=rs.at[slot(h, g)],
                    device_id={"seq": lax.rem(me + 1, seq)}, device_id_type=MESH).wait_recv()

            if per == 1:
                one()
            else:
                pl.when(h * per != me)(one)

    start = lambda c: c.start()
    wait_send = lambda c: c.wait_send()

    def head(h):
        return slice(h * HD, (h + 1) * HD)

    for c in first[:2]:
        c.wait()
    feat = x_v[...].astype(F32)
    scaled = (feat * g_v[...].reshape(1, feat.shape[1])).astype(BF16)
    sq = jnp.sum(feat * feat, axis=1, keepdims=True)
    first[2].wait()
    for c in rest:
        c.start()
    for c in keys:
        c.start()
    first[3].wait()
    first[4].wait()
    low = jnp.dot(scaled, down_v[...], preferred_element_type=F32)
    low_hi = low.astype(BF16)
    low_lo = (low - low_hi.astype(F32)).astype(BF16)
    q_partial = jnp.dot(scaled, w_v[0], preferred_element_type=F32)
    q_partial += jnp.dot(low_hi, up_v[...], preferred_element_type=F32)
    q_partial += jnp.dot(low_lo, up_v[...], preferred_element_type=F32)
    for h in range(heads):
        q_send[h, :, 0:HD] = q_partial[:, head(h)]
        q_send[h, :, HD:PAD] = jnp.broadcast_to(sq, (rows, PAD - HD))
    pl.semaphore_wait(barrier, seq + tensor - 2)
    for g in range(halves):
        to_owners(q_send, q_part, q_ss, q_rs, start, g)

    for c in values:
        c.start()
    wo_load.start()
    paired = per == 1 and seq % 2 == 0
    half = heads // 2
    side = lax.rem(me, jnp.int32(2))
    partner = me + 1 - 2 * side

    def place(h):
        return h % 2 * half + h // 2 if paired else h

    for j in range(2):
        rest[j].wait()
        part = jnp.dot(scaled, w_v[1 + j], preferred_element_type=F32)
        for h in range(heads):
            kv_send[place(h), j, :, 0:HD] = part[:, head(h)]
            kv_send[place(h), j, :, HD:PAD] = jnp.zeros((rows, PAD - HD), F32)

    def scale_of(total):
        return lax.rsqrt(total[:, HD:HD + 1] / INPUT_WIDTH + 1e-05)

    def sum_queries(g):
        at = slice(8 * g, 8 * g + 8)
        q_part[me, at] = q_send[my_h, at]
        wait_parts(q_send, q_part, q_rs, q_ss, g)
        total = q_part[0, at]
        for s in range(1, seq):
            total = total + q_part[s, at]
        scale = scale_of(total)
        lane = lax.broadcasted_iota(jnp.int32, (8, PAD), 1)
        q_all[my_h, at] = jnp.where(lane < HD, total * scale, scale)
        from_owner(q_all, qa_ss, qa_rs, start, g)

    for g in range(halves):
        on_owner(functools.partial(sum_queries, g))

    def pair_parts():
        return pltpu.make_async_remote_copy(
            src_ref=kv_send.at[pl.ds((1 - side) * half, half)], dst_ref=kv_mid,
            send_sem=kvm_ss.at[0], recv_sem=kvm_rs.at[0],
            device_id={"seq": partner}, device_id_type=MESH)

    def pair_sums(d):
        owner_at = lax.rem(me + 2 * d, seq)
        return pltpu.make_async_remote_copy(
            src_ref=kv_sum.at[lax.div(owner_at, jnp.int32(2))],
            dst_ref=kv_part.at[lax.div(me, jnp.int32(2))],
            send_sem=kv_ss.at[d], recv_sem=kv_rs.at[lax.div(me, jnp.int32(2))],
            device_id={"seq": owner_at}, device_id_type=MESH)

    def spread(d):
        to = partner if d == 0 else lax.rem(me + 2 * d, seq)
        return pltpu.make_async_remote_copy(
            src_ref=kv_all.at[me], dst_ref=kv_all.at[me], send_sem=kva_ss.at[d],
            recv_sem=kva_rs.at[me], device_id={"seq": to}, device_id_type=MESH)

    def forward(d):
        h = lax.rem(me + 2 * d, seq)
        return pltpu.make_async_remote_copy(
            src_ref=kv_all.at[h], dst_ref=kv_all.at[h], send_sem=kva_ss.at[half + d - 1],
            recv_sem=kva_rs.at[h], device_id={"seq": partner}, device_id_type=MESH)

    def arrived(h):
        pltpu.make_async_remote_copy(
            src_ref=kv_all.at[h], dst_ref=kv_all.at[h], send_sem=kva_ss.at[0],
            recv_sem=kva_rs.at[h], device_id={"seq": partner}, device_id_type=MESH).wait_recv()

    if paired:
        pair_parts().start()
    else:
        to_owners(kv_send, kv_part, kv_ss, kv_rs, start)

    row = lax.broadcasted_iota(jnp.int32, (group, heads * HD), 0)
    col = lax.broadcasted_iota(jnp.int32, (group, heads * HD), 1)
    low_col = lax.div(row, jnp.int32(NEW)) * HD
    own_head = (col >= low_col) & (col < low_col + HD)

    def fold(full):
        kept = jnp.where(own_head, full, 0.0)
        eight = kept[0:8]
        for i in range(1, group // 8):
            eight = eight + kept[8 * i:8 * i + 8]
        return eight[0:NEW] + eight[NEW:2 * NEW]

    s_row = lax.rem(lax.broadcasted_iota(jnp.int32, (group, span), 0), jnp.int32(NEW))
    position = me * span + lax.broadcasted_iota(jnp.int32, (group, span), 1)
    width = heads * HD

    def weigh(r):
        four = q_full[NEW * r:NEW * (r + 1), :]
        eight = jnp.concatenate([four, four], axis=0)
        tall = jnp.concatenate([eight] * (group // 8), axis=0)
        block = jnp.where(own_head, tall, 0.0).astype(BF16)
        keys[r].wait()
        raw = dot_t(block, k_v[r]) * HD ** (-0.5)
        length = len_ref[r]
        seen = (position < length) & (
            (position < sink_ref[r]) | (length + s_row - position < win_ref[r]))
        scores = jnp.where(seen, raw, NEG)
        top = jnp.max(scores, axis=1, keepdims=True)
        expo = jnp.where(seen, jnp.exp(scores - top), 0.0)
        total = jnp.sum(expo, axis=1, keepdims=True)
        values[r].wait()
        out = jnp.dot(expo.astype(BF16), v_v[r], preferred_element_type=F32)
        return (fold(out), fold(jnp.broadcast_to(top, (group, width))),
                fold(jnp.broadcast_to(total, (group, width))))

    def attend(g):
        at = slice(8 * g, 8 * g + 8)
        wait_results(q_all, qa_ss, qa_rs, g)
        for h in range(heads):
            q_full[at, head(h)] = q_all[h, at, 0:HD]
        pieces = [weigh(each * g + i) for i in range(each)]
        out, top, total = (jnp.concatenate(p, axis=0) for p in zip(*pieces))
        for h in range(heads):
            o_send[h, at, 0:HD] = out[:, head(h)]
            o_send[h, at, HD:HD + SIDE] = top[:, h * HD:h * HD + SIDE]
            o_send[h, at, HD + SIDE:PAD] = total[:, h * HD:h * HD + SIDE]
        to_owners(o_send, o_part, o_ss, o_rs, start, g)

    for c in places:
        c.wait()
    for g in range(halves):
        attend(g)
        if paired and g == 0:
            pair_parts().wait_recv()
            for i in range(half):
                kv_sum[i] = kv_mid[i] + kv_send[side * half + i]
            for d in range(1, half):
                pair_sums(d).start()

    def sum_new():
        if paired:
            kv_part[lax.div(me, jnp.int32(2))] = kv_sum[lax.div(me, jnp.int32(2))]
            for d in range(1, half):
                s = lax.div(lax.rem(me + 2 * d, seq), jnp.int32(2))
                pltpu.make_async_remote_copy(
                    src_ref=kv_sum.at[0], dst_ref=kv_part.at[s], send_sem=kv_ss.at[0],
                    recv_sem=kv_rs.at[s], device_id={"seq": partner},
                    device_id_type=MESH).wait_recv()
        else:
            kv_part[me] = kv_send[my_h]
            wait_parts(kv_send, kv_part, kv_rs, kv_ss)
        scale = q_all[my_h][:, HD:HD + 1]
        for j in range(2):
            total = kv_part[0, j]
            for s in range(1, half if paired else seq):
                total = total + kv_part[s, j]
            kv_all[my_h, j] = total * scale
        if paired:
            for d in range(half):
                spread(d).start()
        else:
            from_owner(kv_all, kva_ss, kva_rs, start)

    on_owner(sum_new)

    def merge(g):
        at = slice(8 * g, 8 * g + 8)
        query = q_all[my_h, at, 0:HD].astype(BF16)
        key = kv_all[my_h, 0, at, 0:HD].astype(BF16)
        value = kv_all[my_h, 1, at, 0:HD].astype(BF16)
        token = lax.broadcasted_iota(jnp.int32, (8, 8), 0)
        other = lax.broadcasted_iota(jnp.int32, (8, 8), 1)
        seen = (lax.div(token, jnp.int32(NEW)) == lax.div(other, jnp.int32(NEW))) & (other <= token)
        fresh = jnp.where(seen, dot_t(query, key) * HD ** (-0.5), NEG)
        own_top = jnp.max(fresh, axis=1, keepdims=True)
        expo = jnp.where(seen, jnp.exp(fresh - own_top), 0.0)
        own_sum = jnp.sum(expo, axis=1, keepdims=True)
        own_out = jnp.dot(expo.astype(BF16), value, preferred_element_type=F32)
        o_part[me, at] = o_send[my_h, at]
        wait_parts(o_send, o_part, o_rs, o_ss, g)
        top = own_top
        for s in range(seq):
            top = jnp.maximum(top, o_part[s, at, HD:HD + 1])
        factor = jnp.exp(own_top - top)
        total = own_sum * factor
        out = own_out * factor
        for s in range(seq):
            piece = o_part[s, at]
            factor = jnp.exp(piece[:, HD:HD + 1] - top)
            out = out + piece[:, 0:HD] * factor
            total = total + piece[:, HD + SIDE:HD + SIDE + 1] * factor
        a_all[my_h, at, 0:HD] = out / total
        a_all[my_h, at, HD:PAD] = jnp.zeros((8, PAD - HD), F32)
        from_owner(a_all, a_ss, a_rs, start, g)

    for g in range(halves):
        on_owner(functools.partial(merge, g))
    if paired:
        for d in range(1, half):
            arrived(lax.rem(me + 2 * d, seq))
            forward(d).start()

    if paired:
        for d in range(half):
            arrived(lax.rem(partner + 2 * d, seq))
    else:
        wait_results(kv_all, kva_ss, kva_rs)
    for h in range(heads):
        for j in range(2):
            kv_ref[j, :, head(h)] = kv_all[h, j, :, 0:HD]
    wo_load.wait()
    for g in range(halves):
        wait_results(a_all, a_ss, a_rs, g)
    for h in range(heads):
        a_full[:, head(h)] = a_all[h, :, 0:HD]
    t_part[mine_t] = dot_t(a_full[...].astype(BF16), wo_v[...])

    def to_tensor(d):
        return pltpu.make_async_remote_copy(
            src_ref=t_part.at[mine_t], dst_ref=t_part.at[mine_t], send_sem=t_ss.at[d],
            recv_sem=t_rs.at[mine_t], device_id={"tensor": lax.rem(mine_t + d, tensor)},
            device_id_type=MESH)

    for d in range(1, tensor):
        to_tensor(d).start()
    for g in range(halves):
        to_owners(q_send, q_part, q_ss, q_rs, wait_send, g)
    for g in range(halves):
        to_owners(o_send, o_part, o_ss, o_rs, wait_send, g)
    for g in range(halves):
        on_owner(functools.partial(from_owner, q_all, qa_ss, qa_rs, wait_send, g))
    if paired:
        pair_parts().wait_send()
        for d in range(1, half):
            pair_sums(d).wait_send()
            forward(d).wait_send()
        for d in range(half):
            spread(d).wait_send()
    else:
        to_owners(kv_send, kv_part, kv_ss, kv_rs, wait_send)
        on_owner(lambda: from_owner(kv_all, kva_ss, kva_rs, wait_send))
    for g in range(halves):
        on_owner(functools.partial(from_owner, a_all, a_ss, a_rs, wait_send, g))
    for d in range(1, tensor):
        s = lax.rem(mine_t + d, tensor)
        pltpu.make_async_remote_copy(
            src_ref=t_part.at[s], dst_ref=t_part.at[s], send_sem=t_ss.at[0], recv_sem=t_rs.at[s],
            device_id={"tensor": s}, device_id_type=MESH).wait_recv()
    mixed = t_part[0]
    for s in range(1, tensor):
        mixed = mixed + t_part[s]
    mixed_ref[...] = mixed
    for d in range(1, tensor):
        to_tensor(d).wait_send()


def shards(
    seq, tensor,
    features, input_norm_scale, query_key_value_weight, adapter_down_weight, adapter_up_weight,
    output_weight, cached_key_rows, cached_value_rows, lengths, sinks, windows,
):
    rows, depth = features.shape
    count, span, width = cached_key_rows.shape
    heads = width // HD
    out_width = output_weight.shape[1]
    weights = jnp.transpose(query_key_value_weight, (1, 0, 2))
    wo = jnp.transpose(output_weight)
    hbm = pl.BlockSpec(memory_space=pltpu.HBM)
    vmem = pl.BlockSpec(memory_space=pltpu.VMEM)

    def like(a):
        return pltpu.VMEM(a.shape, a.dtype)

    dma = lambda n: pltpu.SemaphoreType.DMA((n,))
    ring = max(seq, heads)
    twice = ring * (rows // 8)
    return pl.pallas_call(
        functools.partial(block_kernel, seq, tensor, heads, count),
        out_shape=(
            jax.ShapeDtypeStruct((rows, out_width), F32),
            jax.ShapeDtypeStruct((2, rows, width), F32),
        ),
        in_specs=[hbm] * 11,
        out_specs=(vmem, vmem),
        scratch_shapes=[pltpu.SMEM((count,), jnp.int32)] * 3 + [
            like(features), like(input_norm_scale), like(weights), like(adapter_down_weight),
            like(adapter_up_weight), like(wo), like(cached_key_rows), like(cached_value_rows),
            pltpu.VMEM((heads, rows, PAD), F32),
            pltpu.VMEM((seq, rows, PAD), F32),
            pltpu.VMEM((heads, rows, PAD), F32),
            pltpu.VMEM((rows, width), F32),
            pltpu.VMEM((heads, 2, rows, PAD), F32),
            pltpu.VMEM((heads // 2, 2, rows, PAD), F32),
            pltpu.VMEM((heads // 2, 2, rows, PAD), F32),
            pltpu.VMEM((seq, 2, rows, PAD), F32),
            pltpu.VMEM((heads, 2, rows, PAD), F32),
            pltpu.VMEM((heads, rows, PAD), F32),
            pltpu.VMEM((seq, rows, PAD), F32),
            pltpu.VMEM((heads, rows, PAD), F32),
            pltpu.VMEM((rows, width), F32),
            pltpu.VMEM((tensor, rows, out_width), F32),
            dma(11 + 2 * count),
        ] + [dma(twice)] * 4 + [dma(1)] * 2 + [dma(ring)] * 4 + [dma(twice)] * 4 + [dma(tensor)] * 2,
        compiler_params=pltpu.CompilerParams(
            collective_id=0, has_side_effects=True, vmem_limit_bytes=60 * 1024 * 1024,
        ),
    )(
        features, input_norm_scale, weights, adapter_down_weight, adapter_up_weight, wo,
        cached_key_rows, cached_value_rows, lengths, sinks, windows,
    )


def solution(mesh):
    in_specs = (
        P(None, "seq"),
        P("seq"),
        P("seq", None, "tensor"),
        P("seq", None),
        P(None, "tensor"),
        P("tensor", "seq"),
        P(None, "seq", "tensor"),
        P(None, "seq", "tensor"),
        P(),
        P(),
        P(),
    )
    out_specs = (P(None, "seq"), P(None, None, "tensor"))
    body = functools.partial(shards, mesh.shape["seq"], mesh.shape["tensor"])
    return jax.shard_map(body, mesh=mesh, in_specs=in_specs, out_specs=out_specs, check_vma=False)
```

```python
import functools

import jax
import jax.numpy as jnp
from jax import lax
from jax.experimental import pallas as pl
from jax.experimental.pallas import tpu as pltpu
from jax.sharding import PartitionSpec as P

HD = 224
NEW = 4
INPUT_WIDTH = 7168
PAD = 256
SIDE = 16

NEG = -1e30
CUT = -1e29
MESH = pl.DeviceIdType.MESH
F32 = jnp.float32
BF16 = jnp.bfloat16


def dot_t(a, b):
    return lax.dot_general(a, b, (((1,), (1,)), ((), ())), preferred_element_type=F32)


def block_kernel(
    seq, tensor, heads, count,
    x_hbm, g_hbm, w_hbm, down_hbm, up_hbm, wo_hbm, k_hbm, v_hbm, len_hbm, sink_hbm, win_hbm,
    mixed_ref, kv_ref,
    len_ref, sink_ref, win_ref,
    x_v, g_v, w_v, down_v, up_v, wo_v, k_v, v_v,
    q_send, q_part, q_all, q_full,
    kv_send, kv_mid, kv_sum, kv_part, kv_all,
    o_send, o_part, a_all, a_full, t_part, load_sem,
    q_ss, q_rs, qa_ss, qa_rs, kvm_ss, kvm_rs, kv_ss, kv_rs, kva_ss, kva_rs, o_ss, o_rs, a_ss, a_rs, t_ss, t_rs,
):
    me = lax.axis_index("seq")
    mine_t = lax.axis_index("tensor")
    per = seq // heads
    my_h = lax.div(me, jnp.int32(per))
    owner = lax.rem(me, jnp.int32(per)) == 0
    span = k_v.shape[1]
    rows = x_v.shape[0]
    group = NEW * heads
    halves = rows // 8
    each = count // halves

    def load(src, dst, index):
        return pltpu.make_async_copy(src, dst, load_sem.at[index])

    first = [load(x_hbm, x_v, 0), load(g_hbm, g_v, 1), load(w_hbm.at[0], w_v.at[0], 2),
             load(down_hbm, down_v, 3), load(up_hbm, up_v, 4)]
    rest = [load(w_hbm.at[1], w_v.at[1], 5), load(w_hbm.at[2], w_v.at[2], 6)]
    keys = [load(k_hbm.at[r], k_v.at[r], 8 + r) for r in range(count)]
    values = [load(v_hbm.at[r], v_v.at[r], 8 + count + r) for r in range(count)]
    wo_load = load(wo_hbm, wo_v, 7)
    places = [load(a, b, 8 + 2 * count + i) for i, (a, b) in enumerate(
        ((len_hbm, len_ref), (sink_hbm, sink_ref), (win_hbm, win_ref)))]
    for c in first + places:
        c.start()

    barrier = pltpu.get_barrier_semaphore()
    for d in range(1, seq):
        pl.semaphore_signal(barrier, inc=1, device_id={"seq": lax.rem(me + d, seq)}, device_id_type=MESH)
    for d in range(1, tensor):
        pl.semaphore_signal(barrier, inc=1, device_id={"tensor": lax.rem(mine_t + d, tensor)}, device_id_type=MESH)

    def on_owner(f):
        if per == 1:
            f()
        else:
            pl.when(owner)(f)

    ring = max(seq, heads)

    def view(ref, index, g):
        return ref.at[index] if g is None else ref.at[index, pl.ds(8 * g, 8)]

    def slot(index, g):
        return index if g is None else g * ring + index

    def to_owners(src, dst, ss, rs, act, g=None):
        for d in range(1 if per == 1 else 0, heads):
            h = lax.rem(my_h + d, heads)

            def one(h=h, d=d):
                act(pltpu.make_async_remote_copy(
                    src_ref=view(src, h, g), dst_ref=view(dst, me, g),
                    send_sem=ss.at[slot(d, g)], recv_sem=rs.at[slot(me, g)],
                    device_id={"seq": h * per}, device_id_type=MESH))

            if per == 1:
                one()
            else:
                pl.when(h * per != me)(one)

    def wait_parts(src, dst, rs, ss, g=None):
        for d in range(1, seq):
            s = lax.rem(me + d, seq)
            pltpu.make_async_remote_copy(
                src_ref=view(src, 0, g), dst_ref=view(dst, s, g),
                send_sem=ss.at[0], recv_sem=rs.at[slot(s, g)],
                device_id={"seq": s}, device_id_type=MESH).wait_recv()

    def from_owner(buf, ss, rs, act, g=None):
        for d in range(1, seq):
            act(pltpu.make_async_remote_copy(
                src_ref=view(buf, my_h, g), dst_ref=view(buf, my_h, g),
                send_sem=ss.at[slot(d, g)], recv_sem=rs.at[slot(my_h, g)],
                device_id={"seq": lax.rem(me + d, seq)}, device_id_type=MESH))

    def wait_results(buf, ss, rs, g=None):
        for d in range(1 if per == 1 else 0, heads):
            h = lax.rem(my_h + d, heads)

            def one(h=h):
                pltpu.make_async_remote_copy(
                    src_ref=view(buf, h, g), dst_ref=view(buf, h, g),
                    send_sem=ss.at[0], recv_sem=rs.at[slot(h, g)],
                    device_id={"seq": lax.rem(me + 1, seq)}, device_id_type=MESH).wait_recv()

            if per == 1:
                one()
            else:
                pl.when(h * per != me)(one)

    start = lambda c: c.start()
    wait_send = lambda c: c.wait_send()

    def head(h):
        return slice(h * HD, (h + 1) * HD)

    for c in first[:2]:
        c.wait()
    feat = x_v[...].astype(F32)
    scaled = (feat * g_v[...].reshape(1, feat.shape[1])).astype(BF16)
    sq = jnp.sum(feat * feat, axis=1, keepdims=True)
    first[2].wait()
    for c in rest:
        c.start()
    for c in keys:
        c.start()
    first[3].wait()
    first[4].wait()
    low = jnp.dot(scaled, down_v[...], preferred_element_type=F32)
    low_hi = low.astype(BF16)
    low_lo = (low - low_hi.astype(F32)).astype(BF16)
    q_partial = jnp.dot(scaled, w_v[0], preferred_element_type=F32)
    q_partial += jnp.dot(low_hi, up_v[...], preferred_element_type=F32)
    q_partial += jnp.dot(low_lo, up_v[...], preferred_element_type=F32)
    for h in range(heads):
        q_send[h, :, 0:HD] = q_partial[:, head(h)]
        q_send[h, :, HD:PAD] = jnp.broadcast_to(sq, (rows, PAD - HD))
    pl.semaphore_wait(barrier, seq + tensor - 2)
    for g in range(halves):
        to_owners(q_send, q_part, q_ss, q_rs, start, g)

    for c in values:
        c.start()
    wo_load.start()
    paired = per == 1 and seq % 2 == 0
    half = heads // 2
    side = lax.rem(me, jnp.int32(2))
    partner = me + 1 - 2 * side

    def place(h):
        return h % 2 * half + h // 2 if paired else h

    for j in range(2):
        rest[j].wait()
        part = jnp.dot(scaled, w_v[1 + j], preferred_element_type=F32)
        for h in range(heads):
            kv_send[place(h), j, :, 0:HD] = part[:, head(h)]
            kv_send[place(h), j, :, HD:PAD] = jnp.zeros((rows, PAD - HD), F32)

    def scale_of(total):
        return lax.rsqrt(total[:, HD:HD + 1] / INPUT_WIDTH + 1e-05)

    def sum_queries(g):
        at = slice(8 * g, 8 * g + 8)
        q_part[me, at] = q_send[my_h, at]
        wait_parts(q_send, q_part, q_rs, q_ss, g)
        total = q_part[0, at]
        for s in range(1, seq):
            total = total + q_part[s, at]
        scale = scale_of(total)
        lane = lax.broadcasted_iota(jnp.int32, (8, PAD), 1)
        q_all[my_h, at] = jnp.where(lane < HD, total * scale, scale)
        from_owner(q_all, qa_ss, qa_rs, start, g)

    for g in range(halves):
        on_owner(functools.partial(sum_queries, g))

    def pair_parts():
        return pltpu.make_async_remote_copy(
            src_ref=kv_send.at[pl.ds((1 - side) * half, half)], dst_ref=kv_mid,
            send_sem=kvm_ss.at[0], recv_sem=kvm_rs.at[0],
            device_id={"seq": partner}, device_id_type=MESH)

    def pair_sums(d):
        owner_at = lax.rem(me + 2 * d, seq)
        return pltpu.make_async_remote_copy(
            src_ref=kv_sum.at[lax.div(owner_at, jnp.int32(2))],
            dst_ref=kv_part.at[lax.div(me, jnp.int32(2))],
            send_sem=kv_ss.at[d], recv_sem=kv_rs.at[lax.div(me, jnp.int32(2))],
            device_id={"seq": owner_at}, device_id_type=MESH)

    def spread(d):
        to = partner if d == 0 else lax.rem(me + 2 * d, seq)
        return pltpu.make_async_remote_copy(
            src_ref=kv_all.at[me], dst_ref=kv_all.at[me], send_sem=kva_ss.at[d],
            recv_sem=kva_rs.at[me], device_id={"seq": to}, device_id_type=MESH)

    def forward(d):
        h = lax.rem(me + 2 * d, seq)
        return pltpu.make_async_remote_copy(
            src_ref=kv_all.at[h], dst_ref=kv_all.at[h], send_sem=kva_ss.at[half + d - 1],
            recv_sem=kva_rs.at[h], device_id={"seq": partner}, device_id_type=MESH)

    def arrived(h):
        pltpu.make_async_remote_copy(
            src_ref=kv_all.at[h], dst_ref=kv_all.at[h], send_sem=kva_ss.at[0],
            recv_sem=kva_rs.at[h], device_id={"seq": partner}, device_id_type=MESH).wait_recv()

    if paired:
        pair_parts().start()
    else:
        to_owners(kv_send, kv_part, kv_ss, kv_rs, start)

    row = lax.broadcasted_iota(jnp.int32, (group, heads * HD), 0)
    col = lax.broadcasted_iota(jnp.int32, (group, heads * HD), 1)
    low_col = lax.div(row, jnp.int32(NEW)) * HD
    own_head = (col >= low_col) & (col < low_col + HD)

    def fold(full):
        kept = jnp.where(own_head, full, 0.0)
        eight = kept[0:8]
        for i in range(1, group // 8):
            eight = eight + kept[8 * i:8 * i + 8]
        return eight[0:NEW] + eight[NEW:2 * NEW]

    s_row = lax.rem(lax.broadcasted_iota(jnp.int32, (group, span), 0), jnp.int32(NEW))
    position = me * span + lax.broadcasted_iota(jnp.int32, (group, span), 1)
    width = heads * HD

    def weigh(r):
        four = q_full[NEW * r:NEW * (r + 1), :]
        eight = jnp.concatenate([four, four], axis=0)
        tall = jnp.concatenate([eight] * (group // 8), axis=0)
        block = jnp.where(own_head, tall, 0.0).astype(BF16)
        keys[r].wait()
        raw = dot_t(block, k_v[r]) * HD ** (-0.5)
        length = len_ref[r]
        seen = (position < length) & (
            (position < sink_ref[r]) | (length + s_row - position < win_ref[r]))
        scores = jnp.where(seen, raw, NEG)
        top = jnp.max(scores, axis=1, keepdims=True)
        expo = jnp.where(seen, jnp.exp(scores - top), 0.0)
        total = jnp.sum(expo, axis=1, keepdims=True)
        values[r].wait()
        out = jnp.dot(expo.astype(BF16), v_v[r], preferred_element_type=F32)
        return (fold(out), fold(jnp.broadcast_to(top, (group, width))),
                fold(jnp.broadcast_to(total, (group, width))))

    def attend(g):
        at = slice(8 * g, 8 * g + 8)
        wait_results(q_all, qa_ss, qa_rs, g)
        for h in range(heads):
            q_full[at, head(h)] = q_all[h, at, 0:HD]
        pieces = [weigh(each * g + i) for i in range(each)]
        out, top, total = (jnp.concatenate(p, axis=0) for p in zip(*pieces))
        for h in range(heads):
            o_send[h, at, 0:HD] = out[:, head(h)]
            o_send[h, at, HD:HD + SIDE] = top[:, h * HD:h * HD + SIDE]
            o_send[h, at, HD + SIDE:PAD] = total[:, h * HD:h * HD + SIDE]
        to_owners(o_send, o_part, o_ss, o_rs, start, g)

    for c in places:
        c.wait()
    for g in range(halves):
        attend(g)
        if paired and g == 0:
            pair_parts().wait_recv()
            for i in range(half):
                kv_sum[i] = kv_mid[i] + kv_send[side * half + i]
            for d in range(1, half):
                pair_sums(d).start()

    def sum_new():
        if paired:
            kv_part[lax.div(me, jnp.int32(2))] = kv_sum[lax.div(me, jnp.int32(2))]
            for d in range(1, half):
                s = lax.div(lax.rem(me + 2 * d, seq), jnp.int32(2))
                pltpu.make_async_remote_copy(
                    src_ref=kv_sum.at[0], dst_ref=kv_part.at[s], send_sem=kv_ss.at[0],
                    recv_sem=kv_rs.at[s], device_id={"seq": partner},
                    device_id_type=MESH).wait_recv()
        else:
            kv_part[me] = kv_send[my_h]
            wait_parts(kv_send, kv_part, kv_rs, kv_ss)
        scale = q_all[my_h][:, HD:HD + 1]
        for j in range(2):
            total = kv_part[0, j]
            for s in range(1, half if paired else seq):
                total = total + kv_part[s, j]
            kv_all[my_h, j] = total * scale
        if paired:
            for d in range(half):
                spread(d).start()
        else:
            from_owner(kv_all, kva_ss, kva_rs, start)

    on_owner(sum_new)

    def merge(g):
        at = slice(8 * g, 8 * g + 8)
        query = q_all[my_h, at, 0:HD].astype(BF16)
        key = kv_all[my_h, 0, at, 0:HD].astype(BF16)
        value = kv_all[my_h, 1, at, 0:HD].astype(BF16)
        token = lax.broadcasted_iota(jnp.int32, (8, 8), 0)
        other = lax.broadcasted_iota(jnp.int32, (8, 8), 1)
        seen = (lax.div(token, jnp.int32(NEW)) == lax.div(other, jnp.int32(NEW))) & (other <= token)
        fresh = jnp.where(seen, dot_t(query, key) * HD ** (-0.5), NEG)
        own_top = jnp.max(fresh, axis=1, keepdims=True)
        expo = jnp.where(seen, jnp.exp(fresh - own_top), 0.0)
        own_sum = jnp.sum(expo, axis=1, keepdims=True)
        own_out = jnp.dot(expo.astype(BF16), value, preferred_element_type=F32)
        o_part[me, at] = o_send[my_h, at]
        wait_parts(o_send, o_part, o_rs, o_ss, g)
        top = own_top
        for s in range(seq):
            top = jnp.maximum(top, o_part[s, at, HD:HD + 1])
        factor = jnp.exp(own_top - top)
        total = own_sum * factor
        out = own_out * factor
        for s in range(seq):
            piece = o_part[s, at]
            factor = jnp.exp(piece[:, HD:HD + 1] - top)
            out = out + piece[:, 0:HD] * factor
            total = total + piece[:, HD + SIDE:HD + SIDE + 1] * factor
        a_all[my_h, at, 0:HD] = out / total
        a_all[my_h, at, HD:PAD] = jnp.zeros((8, PAD - HD), F32)
        from_owner(a_all, a_ss, a_rs, start, g)

    for g in range(halves):
        on_owner(functools.partial(merge, g))
    if paired:
        for d in range(1, half):
            arrived(lax.rem(me + 2 * d, seq))
            forward(d).start()

    if paired:
        for d in range(half):
            arrived(lax.rem(partner + 2 * d, seq))
    else:
        wait_results(kv_all, kva_ss, kva_rs)
    for h in range(heads):
        for j in range(2):
            kv_ref[j, :, head(h)] = kv_all[h, j, :, 0:HD]
    wo_load.wait()
    for g in range(halves):
        wait_results(a_all, a_ss, a_rs, g)
    for h in range(heads):
        a_full[:, head(h)] = a_all[h, :, 0:HD]
    t_part[mine_t] = dot_t(a_full[...].astype(BF16), wo_v[...])

    def to_tensor(d):
        return pltpu.make_async_remote_copy(
            src_ref=t_part.at[mine_t], dst_ref=t_part.at[mine_t], send_sem=t_ss.at[d],
            recv_sem=t_rs.at[mine_t], device_id={"tensor": lax.rem(mine_t + d, tensor)},
            device_id_type=MESH)

    for d in range(1, tensor):
        to_tensor(d).start()
    for g in range(halves):
        to_owners(q_send, q_part, q_ss, q_rs, wait_send, g)
    for g in range(halves):
        to_owners(o_send, o_part, o_ss, o_rs, wait_send, g)
    for g in range(halves):
        on_owner(functools.partial(from_owner, q_all, qa_ss, qa_rs, wait_send, g))
    if paired:
        pair_parts().wait_send()
        for d in range(1, half):
            pair_sums(d).wait_send()
            forward(d).wait_send()
        for d in range(half):
            spread(d).wait_send()
    else:
        to_owners(kv_send, kv_part, kv_ss, kv_rs, wait_send)
        on_owner(lambda: from_owner(kv_all, kva_ss, kva_rs, wait_send))
    for g in range(halves):
        on_owner(functools.partial(from_owner, a_all, a_ss, a_rs, wait_send, g))
    for d in range(1, tensor):
        s = lax.rem(mine_t + d, tensor)
        pltpu.make_async_remote_copy(
            src_ref=t_part.at[s], dst_ref=t_part.at[s], send_sem=t_ss.at[0], recv_sem=t_rs.at[s],
            device_id={"tensor": s}, device_id_type=MESH).wait_recv()
    mixed = t_part[0]
    for s in range(1, tensor):
        mixed = mixed + t_part[s]
    mixed_ref[...] = mixed
    for d in range(1, tensor):
        to_tensor(d).wait_send()


def place_kernel(mixed_hbm, kv_hbm, mixed_out, kv_out, sem):
    copies = [pltpu.make_async_copy(kv_hbm.at[j], kv_out.at[j], sem.at[j]) for j in range(2)]
    copies.append(pltpu.make_async_copy(mixed_hbm, mixed_out, sem.at[2]))
    for c in copies:
        c.start()
    for c in copies:
        c.wait()


def shards(
    seq, tensor,
    features, input_norm_scale, query_key_value_weight, adapter_down_weight, adapter_up_weight,
    output_weight, cached_key_rows, cached_value_rows, lengths, sinks, windows,
):
    rows, depth = features.shape
    count, span, width = cached_key_rows.shape
    heads = width // HD
    out_width = output_weight.shape[1]
    weights = jnp.transpose(query_key_value_weight, (1, 0, 2))
    wo = jnp.transpose(output_weight)
    hbm = pl.BlockSpec(memory_space=pltpu.HBM)
    vmem = pl.BlockSpec(memory_space=pltpu.VMEM)

    def like(a):
        return pltpu.VMEM(a.shape, a.dtype)

    dma = lambda n: pltpu.SemaphoreType.DMA((n,))
    ring = max(seq, heads)
    twice = ring * (rows // 8)
    mixed, new_kv = pl.pallas_call(
        functools.partial(block_kernel, seq, tensor, heads, count),
        out_shape=(
            jax.ShapeDtypeStruct((rows, out_width), F32),
            jax.ShapeDtypeStruct((2, rows, width), F32),
        ),
        in_specs=[hbm] * 11,
        out_specs=(vmem, vmem),
        scratch_shapes=[pltpu.SMEM((count,), jnp.int32)] * 3 + [
            like(features), like(input_norm_scale), like(weights), like(adapter_down_weight),
            like(adapter_up_weight), like(wo), like(cached_key_rows), like(cached_value_rows),
            pltpu.VMEM((heads, rows, PAD), F32),
            pltpu.VMEM((seq, rows, PAD), F32),
            pltpu.VMEM((heads, rows, PAD), F32),
            pltpu.VMEM((rows, width), F32),
            pltpu.VMEM((heads, 2, rows, PAD), F32),
            pltpu.VMEM((heads // 2, 2, rows, PAD), F32),
            pltpu.VMEM((heads // 2, 2, rows, PAD), F32),
            pltpu.VMEM((seq, 2, rows, PAD), F32),
            pltpu.VMEM((heads, 2, rows, PAD), F32),
            pltpu.VMEM((heads, rows, PAD), F32),
            pltpu.VMEM((seq, rows, PAD), F32),
            pltpu.VMEM((heads, rows, PAD), F32),
            pltpu.VMEM((rows, width), F32),
            pltpu.VMEM((tensor, rows, out_width), F32),
            dma(11 + 2 * count),
        ] + [dma(twice)] * 4 + [dma(1)] * 2 + [dma(ring)] * 4 + [dma(twice)] * 4 + [dma(tensor)] * 2,
        compiler_params=pltpu.CompilerParams(
            collective_id=0, has_side_effects=True, vmem_limit_bytes=60 * 1024 * 1024,
        ),
    )(
        features, input_norm_scale, weights, adapter_down_weight, adapter_up_weight, wo,
        cached_key_rows, cached_value_rows, lengths, sinks, windows,
    )
    return pl.pallas_call(
        place_kernel,
        out_shape=(
            jax.ShapeDtypeStruct(mixed.shape, F32), jax.ShapeDtypeStruct(new_kv.shape, F32)),
        in_specs=[hbm] * 2,
        out_specs=(hbm, hbm),
        scratch_shapes=[dma(3)],
        compiler_params=pltpu.CompilerParams(vmem_limit_bytes=60 * 1024 * 1024),
    )(mixed, new_kv)


def solution(mesh):
    in_specs = (
        P(None, "seq"),
        P("seq"),
        P("seq", None, "tensor"),
        P("seq", None),
        P(None, "tensor"),
        P("tensor", "seq"),
        P(None, "seq", "tensor"),
        P(None, "seq", "tensor"),
        P(),
        P(),
        P(),
    )
    out_specs = (P(None, "seq"), P(None, None, "tensor"))
    body = functools.partial(shards, mesh.shape["seq"], mesh.shape["tensor"])
    return jax.shard_map(body, mesh=mesh, in_specs=in_specs, out_specs=out_specs, check_vma=False)
```
